512 devices in a mesh: ens: 8 (over z_lo), lat: 4 (over z_hi, core), lon: 16 (over x, y).
Axes of the slice: x: 4, y: 4, z: 16 (z_hi: 2, z_lo: 8; z = z_hi * 8 + z_lo), core: 2. Of those that a mesh axis runs over, the one named last changes fastest.
Arguments:
- grad_tokens: bfloat16 [104, 131072], P(None, ('lat', 'lon')), may hold values from -6 to 6
- token_index: int32 [64, 2048], P('lat', 'lon'), may hold values from 0 to 131071, as said below
- members: bfloat16 [16, 104, 64, 2048], P('ens', None, 'lat', 'lon'), may hold values from -6 to 6
- lat_taps: float32 [17], replicated, may hold values from 0.05 to 1
- lon_taps: float32 [17], replicated, may hold values from 0.05 to 1
Outputs:
- increment: float32 [104, 64, 2048], P('ens', 'lat', 'lon')
The draws below stay inside these ranges and needn't reach their ends.
Inputs may be any that keep to these rules, and one draw needn't show every extreme that they name: `token_index`: every token is the token of exactly one cell. With grid blocks numbered b = (latitude block) * (longitude blocks) + (longitude block), each of 16 x 128 cells, the cells of block b that take tokens from s * 2048 .. (s + 1) * 2048 - 1 take exactly the tokens s * 2048 + b * 32 + k for k = 0 .. 31, in any order over the block's cells.
All inputs are finite; a program needn't handle non-finite values.
Results may differ from the reference program's by a relative error of at most 0.0003.
Values may be sent and summed in bfloat16 or wider, within the bound.
A program may use at most 64 MiB of HBM per device.

```python
import math
import jax
import jax.numpy as jnp
from jax import lax

HALO = 8
LAT_DEV = 16
LON_DEV = 128
CHANNELS = 104
NLAT = 64
NLON = 2048
TOKENS = 131072
MEMBERS = 16
TAPS = 17


def draw_token_index(key, part):
    blocks_lat = NLAT // LAT_DEV
    blocks_lon = NLON // LON_DEV
    blocks = blocks_lat * blocks_lon
    cells = LAT_DEV * LON_DEV
    piece = cells // blocks
    keys = jax.random.split(key, blocks)
    orders = jax.vmap(lambda k: jax.random.permutation(k, cells))(keys).astype(jnp.int32)
    block_ids = jnp.arange(blocks, dtype=jnp.int32)[:, None]
    source = orders // piece
    within = orders % piece
    token = source * cells + block_ids * piece + within
    token = token.reshape(blocks_lat, blocks_lon, LAT_DEV, LON_DEV)
    token = jnp.transpose(token, (0, 2, 1, 3)).reshape(NLAT, NLON)
    return token.astype(jnp.int32)


def block_scale(rng, dims, pieces, least, largest):
    loudness = 1.0
    for position, parts in pieces:
        draws = jax.random.uniform(jax.random.fold_in(jax.random.fold_in(rng, 6), position), (parts,), jnp.float32, least / len(pieces), largest / len(pieces))
        loudness = loudness * jnp.repeat(jnp.exp(draws), dims[position] // parts).reshape((-1,) + (1,) * (len(dims) - 1 - position))
    return loudness


def noise(rng, shape, scale, most, pieces=(), kind=jnp.bfloat16):
    level = block_scale(rng, shape, pieces, -0.22, 0.18) if pieces else 1.0
    entries = jax.random.normal(rng, shape, jnp.float32) * scale * level
    return jnp.minimum(jnp.maximum(entries, -most), most).astype(kind)


def setup_inputs(seed: int = 0) -> dict:
    splits = jax.random.split(jax.random.key(seed), 6)
    return {
        "grad_tokens": noise(splits[0], (CHANNELS, TOKENS), 1.0, 6.0, ((1, 64),)),
        "token_index": draw_token_index(jax.random.fold_in(splits[5], 71), 0),
        "members": noise(splits[2], (MEMBERS, CHANNELS, NLAT, NLON), 1.0, 6.0, ((0, 8), (2, 4), (3, 16))),
        "lat_taps": jnp.clip(jnp.exp(jax.random.uniform(splits[3], (TAPS,), jnp.float32, math.log(0.05), math.log(1.0))), 0.05, 1.0),
        "lon_taps": jnp.clip(jnp.exp(jax.random.uniform(splits[4], (TAPS,), jnp.float32, math.log(0.05), math.log(1.0))), 0.05, 1.0),
    }


def lat_smooth(field, taps):
    upper = jnp.arange(NLAT, dtype=jnp.int32)[:, None]
    lower = jnp.arange(NLAT, dtype=jnp.int32)[None, :]
    offset = upper - lower + HALO
    inside = (offset >= 0) & (offset <= 2 * HALO)
    matrix = jnp.where(inside, taps[jnp.clip(offset, 0, 2 * HALO)], 0.0)
    return jnp.einsum("cul,ui->cil", field, matrix, precision=lax.Precision.HIGHEST)


def lon_smooth(field, taps):
    total = jnp.zeros_like(field)
    for shift in range(-HALO, HALO + 1):
        total = total + taps[shift + HALO] * jnp.roll(field, -shift, axis=2)
    return total


def localize(field, lat_w, lon_w):
    return lon_smooth(lat_smooth(field, lat_w), lon_w)


def reference(grad_tokens, token_index, members, lat_taps, lon_taps):
    grid = jnp.take(grad_tokens, token_index.reshape(-1).astype(jnp.int32), axis=1)
    grid = grid.reshape(CHANNELS, NLAT, NLON).astype(jnp.float32)
    lat_back = lat_taps[::-1]
    lon_back = lon_taps[::-1]

    def one_member(total, member):
        member = member.astype(jnp.float32)
        control = localize(member * grid, lat_back, lon_back)
        return total + member * localize(control, lat_taps, lon_taps), None

    start = jnp.zeros((CHANNELS, NLAT, NLON), jnp.float32)
    total, _ = lax.scan(one_member, start, members)
    return total / (MEMBERS - 1)
```

```python
import functools

import jax
import jax.numpy as jnp
from jax import lax
from jax.experimental import pallas as pl
from jax.experimental.pallas import tpu as pltpu
from jax.sharding import PartitionSpec as P

MESH = pl.DeviceIdType.MESH
BF16, F32 = jnp.bfloat16, jnp.float32
FIRST = (0, 4, 7, 10)
COUNT = (4, 3, 3, 3)
GROUP = 13
SLOTS = 4
ENS, LAT, LON = 8, 4, 16
ROWS, COLS = 16, 128
TALL = LAT * ROWS
HALO = 8
REACH = 2 * HALO
PIECE = 32
VMEM = pl.BlockSpec(memory_space=pltpu.VMEM)
ANY = pl.BlockSpec(memory_space=pl.ANY)
SMEM = pl.BlockSpec(memory_space=pltpu.SMEM)


def position():
    return lax.axis_index("ens"), lax.axis_index("lat"), lax.axis_index("lon")


def remote(src, dst, send, recv, device):
    return pltpu.make_async_remote_copy(
        src_ref=src, dst_ref=dst, send_sem=send, recv_sem=recv, device_id=device, device_id_type=MESH
    )


def first_of(lat):
    return jnp.where(lat == 0, 0, 3 * lat + 1)


def scatter_kernel(
    members, tok, index, order, moved_m, moved_t, moved_i,
    tile, sorted_t, m_send, m_recv, t_send, t_recv, u_send, u_recv, i_send, i_recv, own_sem,
):
    e, l, n = position()
    barrier = pltpu.get_barrier_semaphore()
    for de in range(ENS):
        for q in range(LAT):
            who = (lax.rem(e + de, ENS), q, n)
            if de == 0:

                @pl.when(l != q)
                def _():
                    pl.semaphore_signal(barrier, inc=1, device_id=who, device_id_type=MESH)
            else:
                pl.semaphore_signal(barrier, inc=1, device_id=who, device_id_type=MESH)
    for dn in range(1, LON):
        pl.semaphore_signal(barrier, inc=1, device_id=(e, l, lax.rem(n + dn, LON)), device_id_type=MESH)
    block = l * LON + n
    wanted = index[...]
    offset = (wanted >> 11) * PIECE + (wanted & 2047) - block * PIECE
    moved_i[l] = offset
    tile[n] = tok[n]

    @pl.when(l != 0)
    def _():
        moved_m[:, SLOTS - 1] = jnp.zeros((2 * ENS, LAT, ROWS, COLS), BF16)

    pl.semaphore_wait(barrier, ENS * LAT - 1 + LON - 1)

    def token_copy(dn):
        to = lax.rem(n + dn, LON)
        return remote(tok.at[to], tile.at[n], t_send.at[dn], t_recv.at[n], (e, l, to))

    for dn in range(1, LON):
        token_copy(dn).start()

    def index_copy(q):
        return remote(moved_i.at[l], moved_i.at[l], i_send.at[q], i_recv.at[l], (e, q, n))

    for q in range(LAT):

        @pl.when(l != q)
        def _():
            index_copy(q).start()

    def member_copy(de, q):
        to = lax.rem(e + de, ENS)
        return remote(
            members.at[:, pl.ds(GROUP * to + FIRST[q], COUNT[q])],
            moved_m.at[pl.ds(2 * e, 2), pl.ds(0, COUNT[q]), l],
            m_send.at[LAT * de + q],
            m_recv.at[LAT * e + l],
            (to, q, n),
        )

    def own_copy(q):
        return pltpu.make_async_copy(
            members.at[:, pl.ds(GROUP * e + FIRST[q], COUNT[q])],
            moved_m.at[pl.ds(2 * e, 2), pl.ds(0, COUNT[q]), l],
            own_sem.at[0],
        )

    for de in (4, 3, 5, 2, 6, 1, 7, 0):
        for q in range(LAT):
            if de == 0:

                @pl.when(l != q)
                def _():
                    member_copy(de, q).start()

                @pl.when(l == q)
                def _():
                    own_copy(q).start()
            else:
                member_copy(de, q).start()

    for dn in range(1, LON):
        frm = lax.rem(n + dn, LON)
        remote(tok.at[frm], tile.at[frm], t_send.at[dn], t_recv.at[frm], (e, l, frm)).wait_recv()
    flat = tile[...].reshape(LON * 16, COLS)
    sorted_t[...] = (
        jnp.dot(order[...], flat, preferred_element_type=F32).astype(BF16).reshape(LAT, 64, COLS)
    )
    moved_t[l] = sorted_t[l]

    def sorted_copy(q):
        return remote(sorted_t.at[q], moved_t.at[l], u_send.at[q], u_recv.at[l], (e, q, n))

    for q in range(LAT):

        @pl.when(l != q)
        def _():
            sorted_copy(q).start()

    for q in range(LAT):

        @pl.when(l != q)
        def _():
            remote(sorted_t.at[q], moved_t.at[q], u_send.at[q], u_recv.at[q], (e, q, n)).wait_recv()
            remote(moved_i.at[q], moved_i.at[q], i_send.at[q], i_recv.at[q], (e, q, n)).wait_recv()
            sorted_copy(q).wait_send()
            index_copy(q).wait_send()
    for dn in range(1, LON):
        token_copy(dn).wait_send()

    def arrival(frm, q, count):
        ref = moved_m.at[pl.ds(2 * frm, 2), pl.ds(0, count), q]
        return remote(ref, ref, m_send.at[0], m_recv.at[LAT * frm + q], (frm, q, n))

    for de in range(ENS):
        frm = lax.rem(e + de, ENS)
        for q in range(LAT):
            away = (l != q) if de == 0 else True

            @pl.when(jnp.logical_and(away, l == 0))
            def _():
                arrival(frm, q, COUNT[0]).wait_recv()

            @pl.when(jnp.logical_and(away, l != 0))
            def _():
                arrival(frm, q, COUNT[1]).wait_recv()

            if de == 0:

                @pl.when(l != q)
                def _():
                    member_copy(de, q).wait_send()

                @pl.when(l == q)
                def _():
                    own_copy(q).wait()
            else:
                member_copy(de, q).wait_send()


def scatter(members, tok, index, order):
    dma = pltpu.SemaphoreType.DMA
    return pl.pallas_call(
        scatter_kernel,
        out_shape=(
            jax.ShapeDtypeStruct((2 * ENS, SLOTS, LAT, ROWS, COLS), BF16),
            jax.ShapeDtypeStruct((LAT, 64, COLS), BF16),
            jax.ShapeDtypeStruct((LAT, ROWS, COLS), jnp.int32),
        ),
        in_specs=[ANY, VMEM, VMEM, VMEM],
        out_specs=(VMEM, VMEM, VMEM),
        scratch_shapes=[
            pltpu.VMEM((LON, 16, COLS), BF16),
            pltpu.VMEM((LAT, 64, COLS), BF16),
            dma((ENS * LAT,)), dma((ENS * LAT,)),
            dma((LON,)), dma((LON,)),
            dma((LAT,)), dma((LAT,)),
            dma((LAT,)), dma((LAT,)),
            dma((1,)),
        ],
        compiler_params=pltpu.CompilerParams(
            collective_id=0, has_side_effects=True, vmem_limit_bytes=40 * 2**20
        ),
    )(members, tok, index, order)


def iota(shape, dim):
    return lax.broadcasted_iota(jnp.int32, shape, dim)


def split(x):
    hi = x.astype(BF16)
    return hi, (x - hi.astype(F32)).astype(BF16)


def matrices(lat_taps, lon_taps, lat_hi, lat_lo, own_w, edge_hi, edge_lo):
    taps = [lat_taps[p] for p in range(2 * HALO + 1)]
    shift = iota((TALL, TALL), 1) - iota((TALL, TALL), 0) + HALO
    once = jnp.zeros((TALL, TALL), F32)
    for p, tap in enumerate(taps):
        once = jnp.where(shift == p, tap, once)
    both = lax.dot_general(
        once, once, (((1,), (1,)), ((), ())), precision=lax.Precision.HIGHEST, preferred_element_type=F32
    )
    hi, lo = split(both)
    lat_hi[...] = jnp.zeros_like(lat_hi)
    lat_lo[...] = jnp.zeros_like(lat_lo)
    for j in range(4):
        lat_hi[j * TALL : (j + 1) * TALL, j * TALL : (j + 1) * TALL] = hi
        lat_lo[j * TALL : (j + 1) * TALL, j * TALL : (j + 1) * TALL] = lo
    taps = [lon_taps[p] for p in range(2 * HALO + 1)]
    twice = []
    for d in range(REACH + 1):
        total = taps[d] * taps[0]
        for a in range(d + 1, REACH + 1):
            total = total + taps[a] * taps[a - d]
        twice.append(total)

    def band(distance):
        out = jnp.zeros(distance.shape, F32)
        for d in range(REACH + 1):
            out = jnp.where(distance == d, twice[d], out)
        return split(out)

    hi, lo = band(jnp.abs(iota((COLS, COLS), 0) - iota((COLS, COLS), 1)))
    own_w[0:COLS, 0:COLS] = hi
    own_w[COLS:, 0:COLS] = hi
    own_w[0:COLS, COLS:] = lo
    own_w[COLS:, COLS:] = jnp.zeros_like(lo)
    edge_hi[...] = jnp.zeros_like(edge_hi)
    edge_lo[...] = jnp.zeros_like(edge_lo)
    for side in range(2):
        start = -REACH if side == 0 else COLS
        hi, lo = band(jnp.abs(iota((REACH, COLS), 0) + start - iota((REACH, COLS), 1)))
        for j in range(8):
            rows = slice(side * COLS + j * REACH, side * COLS + (j + 1) * REACH)
            edge_hi[rows, j * COLS : (j + 1) * COLS] = hi
            edge_lo[rows, j * COLS : (j + 1) * COLS] = lo


def gather_kernel(
    moved_m, moved_t, moved_i, pack, spread, lat_taps, lon_taps,
    grid, edge_m, edge_g, lat_hi, lat_lo, own_w, edge_hi, edge_lo, lanes,
):
    matrices(lat_taps, lon_taps, lat_hi, lat_lo, own_w, edge_hi, edge_lo)
    parts = [moved_t[:, 16 * j : 16 * j + 16, :].astype(F32).reshape(64, COLS) for j in range(4)]
    lane = iota((64, COLS), 1) // PIECE
    for l in range(LAT):
        total = jnp.zeros((64, COLS), F32)
        for j in range(4):
            turned = parts[j] if j == l else pltpu.roll(parts[j], (j - l) * PIECE % COLS, 1)
            total = jnp.where(lane == j, turned, total)
        lanes[l] = total
    high = iota((8, COLS), 0) // 4
    for l in range(LAT):

        @pl.loop(0, ROWS)
        def _(i):
            offset = jnp.broadcast_to(moved_i[l, pl.ds(i, 1), :], (8, COLS))
            which = (offset >> 7) - high
            at = offset & 127
            total = jnp.zeros((8, COLS), F32)
            for v in range(8):
                found = jnp.take_along_axis(lanes[l, 8 * v : 8 * v + 8, :], at, axis=1)
                total = jnp.where(which == 2 * v, found, total)
            total = total[0:4] + total[4:8]
            for c in range(SLOTS):
                grid[c, pl.ds(l * ROWS + i, 1), :] = total[c : c + 1]

    for c in range(SLOTS):
        out = jnp.dot(grid[c].astype(BF16), spread[...], preferred_element_type=F32).astype(BF16)
        edge_g[0, c] = out[:, :COLS]
        edge_g[1, c] = out[:, COLS:]
        for half in range(2):
            row = jnp.concatenate(
                [moved_m[8 * half + j, c].reshape(TALL, COLS) for j in range(8)], axis=1
            )
            out = jnp.dot(row, pack[...], preferred_element_type=F32).astype(BF16)
            edge_m[0, 2 * c + half] = out[:, :COLS]
            edge_m[1, 2 * c + half] = out[:, COLS:]


def gathered(moved_m, moved_t, moved_i, pack, spread, lat_taps, lon_taps):
    s = jax.ShapeDtypeStruct
    return pl.pallas_call(
        gather_kernel,
        out_shape=(
            s((SLOTS, TALL, COLS), F32),
            s((2, 2 * SLOTS, TALL, COLS), BF16),
            s((2, SLOTS, TALL, COLS), BF16),
            s((256, 256), BF16), s((256, 256), BF16), s((256, 256), BF16),
            s((256, 1024), BF16), s((256, 1024), BF16),
        ),
        in_specs=[VMEM] * 5 + [SMEM] * 2,
        out_specs=(VMEM,) * 8,
        scratch_shapes=[pltpu.VMEM((LAT, 64, COLS), F32)],
        compiler_params=pltpu.CompilerParams(vmem_limit_bytes=40 * 2**20),
    )(moved_m, moved_t, moved_i, pack, spread, lat_taps, lon_taps)


def edge_kernel(edge_m, edge_g, near_m, near_g, send, recv):
    e, l, n = position()
    barrier = pltpu.get_barrier_semaphore()
    whom = [lax.rem(n + LON - 1, LON), lax.rem(n + 1, LON)]
    for to in whom:
        pl.semaphore_signal(barrier, inc=1, device_id=(e, l, to), device_id_type=MESH)
    pl.semaphore_wait(barrier, 2)
    copies = []
    for side in range(2):
        dev = (e, l, whom[side])
        copies.append(remote(edge_g.at[side], near_g.at[1 - side], send.at[side], recv.at[side], dev))
        copies.append(remote(edge_m.at[side], near_m.at[1 - side], send.at[2 + side], recv.at[2 + side], dev))
    for c in copies:
        c.start()
    for c in copies:
        c.wait()


def exchanged(edge_m, edge_g):
    s = jax.ShapeDtypeStruct
    return pl.pallas_call(
        edge_kernel,
        out_shape=(s(edge_m.shape, BF16), s(edge_g.shape, BF16)),
        in_specs=[VMEM] * 2,
        out_specs=(VMEM, VMEM),
        scratch_shapes=[pltpu.SemaphoreType.DMA((4,)), pltpu.SemaphoreType.DMA((4,))],
        compiler_params=pltpu.CompilerParams(
            collective_id=1, has_side_effects=True, vmem_limit_bytes=40 * 2**20
        ),
    )(edge_m, edge_g)


def local_kernel(moved_m, grid, near_m, near_g, lat_hi, lat_lo, own_w, edge_hi, edge_lo, out):
    def dot(a, b):
        return jnp.dot(a, b, preferred_element_type=F32)

    for c in range(SLOTS):
        g = grid[c]
        sides = [near_g[side, c].astype(F32) for side in range(2)]
        total = jnp.zeros((TALL, COLS), F32)
        for half in range(2):
            his, los = [], []
            for side in range(2):
                hi, lo = split(near_m[side, 2 * c + half].astype(F32) * sides[side])
                his.append(hi)
                los.append(lo)
            hi, lo = jnp.concatenate(his, axis=1), jnp.concatenate(los, axis=1)
            outer = dot(hi, edge_hi[...]) + dot(lo, edge_hi[...]) + dot(hi, edge_lo[...])
            z_hi, z_lo = [], []
            for j in range(8):
                m = moved_m[8 * half + j, c].reshape(TALL, COLS).astype(F32)
                hi, lo = split(m * g)
                both = dot(jnp.concatenate([hi, lo], axis=1), own_w[...])
                z = both[:, :COLS] + both[:, COLS:] + outer[:, j * COLS : (j + 1) * COLS]
                hi, lo = split(z)
                z_hi.append(hi)
                z_lo.append(lo)

            def field_pairs(parts):
                return jnp.concatenate(
                    [jnp.concatenate(parts[0:4], axis=0), jnp.concatenate(parts[4:8], axis=0)], axis=1
                )

            z_hi, z_lo = field_pairs(z_hi), field_pairs(z_lo)
            v = dot(lat_hi[...], z_hi) + dot(lat_lo[...], z_hi) + dot(lat_hi[...], z_lo)
            for j in range(8):
                m = moved_m[8 * half + j, c].reshape(TALL, COLS).astype(F32)
                k = j % 4
                total = total + m * v[k * TALL : (k + 1) * TALL, (j // 4) * COLS : (j // 4 + 1) * COLS]
        total = total / (2 * ENS - 1)
        for l in range(LAT):
            out[l, c] = total[l * ROWS : (l + 1) * ROWS]


def localized(*args):
    return pl.pallas_call(
        local_kernel,
        out_shape=jax.ShapeDtypeStruct((LAT, SLOTS, ROWS, COLS), F32),
        in_specs=[VMEM] * 9,
        out_specs=VMEM,
        compiler_params=pltpu.CompilerParams(vmem_limit_bytes=40 * 2**20),
    )(*args)


def return_kernel(part, out, send, recv):
    e, l, n = position()
    barrier = pltpu.get_barrier_semaphore()
    for q in range(LAT):

        @pl.when(l != q)
        def _():
            pl.semaphore_signal(barrier, inc=1, device_id=(e, q, n), device_id_type=MESH)

    pl.semaphore_wait(barrier, LAT - 1)

    def copy(src, q, count):
        return remote(
            part.at[q, pl.ds(0, count)], out.at[pl.ds(first_of(l), count)], send.at[q], recv.at[l], (e, q, n)
        )

    for q in range(LAT):
        for src in range(2):

            @pl.when(jnp.logical_and(l != q, (l != 0) if src else (l == 0)))
            def _():
                copy(src, q, COUNT[src]).start()

    for src in range(2):

        @pl.when((l != 0) if src else (l == 0))
        def _():
            out[pl.ds(first_of(l), COUNT[src])] = part[l, 0 : COUNT[src]]

    for q in range(LAT):

        @pl.when(l != q)
        def _():
            ref = out.at[pl.ds(FIRST[q], COUNT[q])]
            remote(ref, ref, send.at[q], recv.at[q], (e, q, n)).wait_recv()

        for src in range(2):

            @pl.when(jnp.logical_and(l != q, (l != 0) if src else (l == 0)))
            def _():
                copy(src, q, COUNT[src]).wait_send()


def returned(part):
    return pl.pallas_call(
        return_kernel,
        out_shape=jax.ShapeDtypeStruct((GROUP, ROWS, COLS), F32),
        in_specs=[VMEM],
        out_specs=VMEM,
        scratch_shapes=[pltpu.SemaphoreType.DMA((LAT,)), pltpu.SemaphoreType.DMA((LAT,))],
        compiler_params=pltpu.CompilerParams(collective_id=2, has_side_effects=True),
    )(part)


def selections():
    to, frm = jnp.arange(256)[:, None], jnp.arange(256)[None, :]
    q, j, g, ch = to // 64, to // 16 % 4, to // 4 % 4, to % 4
    order = (frm == (4 * g + j) * 16 + 4 * q + ch).astype(BF16)
    row, col = jnp.arange(1024)[:, None], jnp.arange(256)[None, :]
    side, j, cc = col // COLS, col % COLS // REACH, col % REACH
    edge = jnp.where(side == 0, cc, COLS - REACH + cc)
    pack = (row == j * COLS + edge).astype(BF16)
    spread = (jnp.arange(COLS)[:, None] == edge).astype(BF16)
    return order, pack, spread


def local(grad_tokens, token_index, members, lat_taps, lon_taps):
    e = lax.axis_index("ens")
    mine = lax.dynamic_slice_in_dim(grad_tokens, GROUP * e, GROUP, axis=0)
    rows = [FIRST[q] + min(c, COUNT[q] - 1) for q in range(LAT) for c in range(SLOTS)]
    mine = jnp.concatenate([mine[r : r + 1] for r in rows], axis=0)
    tok = mine.reshape(16, LAT, LON, PIECE).transpose(2, 0, 1, 3).reshape(LON, 16, COLS)
    order, pack, spread = selections()
    moved_m, moved_t, moved_i = scatter(members, tok, token_index, order)
    grid, edge_m, edge_g, *mats = gathered(moved_m, moved_t, moved_i, pack, spread, lat_taps, lon_taps)
    near_m, near_g = exchanged(edge_m, edge_g)
    part = localized(moved_m, grid, near_m, near_g, *mats)
    return returned(part)


def solution(mesh):
    in_specs = (P(None, ("lat", "lon")), P("lat", "lon"), P("ens", None, "lat", "lon"), P(), P())
    out_specs = P("ens", "lat", "lon")
    return jax.shard_map(local, mesh=mesh, in_specs=in_specs, out_specs=out_specs, check_vma=False)
```

```python
import functools

import jax
import jax.numpy as jnp
from jax import lax
from jax.experimental import pallas as pl
from jax.experimental.pallas import tpu as pltpu
from jax.sharding import PartitionSpec as P

MESH = pl.DeviceIdType.MESH
BF16, F32 = jnp.bfloat16, jnp.float32
FIRST = (0, 4, 7, 10)
COUNT = (4, 3, 3, 3)
CHANNELS = 104
GROUP = 13
SLOTS = 4
PART_FIRST = (0, 2)
PART_COUNT = ((2, 2, 2, 2), (2, 1, 1, 1))
ENS, LAT, LON = 8, 4, 16
ROWS, COLS = 16, 128
TALL = LAT * ROWS
HALO = 8
REACH = 2 * HALO
PIECE = 32
VMEM = pl.BlockSpec(memory_space=pltpu.VMEM)
ANY = pl.BlockSpec(memory_space=pl.ANY)
SMEM = pl.BlockSpec(memory_space=pltpu.SMEM)


def position():
    return lax.axis_index("ens"), lax.axis_index("lat"), lax.axis_index("lon")


def remote(src, dst, send, recv, device):
    return pltpu.make_async_remote_copy(
        src_ref=src, dst_ref=dst, send_sem=send, recv_sem=recv, device_id=device, device_id_type=MESH
    )


def first_of(lat):
    return jnp.where(lat == 0, 0, 3 * lat + 1)


def iota(shape, dim):
    return lax.broadcasted_iota(jnp.int32, shape, dim)


def split(x):
    hi = x.astype(BF16)
    return hi, (x - hi.astype(F32)).astype(BF16)


def matrices(lat_taps, lon_taps, lat_hi, lat_lo, own_w, edge_hi, edge_lo):
    taps = [lat_taps[p] for p in range(2 * HALO + 1)]
    shift = iota((TALL, TALL), 1) - iota((TALL, TALL), 0) + HALO
    once = jnp.zeros((TALL, TALL), F32)
    for p, tap in enumerate(taps):
        once = jnp.where(shift == p, tap, once)
    both = lax.dot_general(
        once, once, (((1,), (1,)), ((), ())), precision=lax.Precision.HIGHEST, preferred_element_type=F32
    )
    hi, lo = split(both)
    lat_hi[...] = jnp.zeros_like(lat_hi)
    lat_lo[...] = jnp.zeros_like(lat_lo)
    for j in range(4):
        lat_hi[j * TALL : (j + 1) * TALL, j * TALL : (j + 1) * TALL] = hi
        lat_lo[j * TALL : (j + 1) * TALL, j * TALL : (j + 1) * TALL] = lo
    taps = [lon_taps[p] for p in range(2 * HALO + 1)]
    twice = []
    for d in range(REACH + 1):
        total = taps[d] * taps[0]
        for a in range(d + 1, REACH + 1):
            total = total + taps[a] * taps[a - d]
        twice.append(total)

    def band(distance):
        out = jnp.zeros(distance.shape, F32)
        for d in range(REACH + 1):
            out = jnp.where(distance == d, twice[d], out)
        return split(out)

    hi, lo = band(jnp.abs(iota((COLS, COLS), 0) - iota((COLS, COLS), 1)))
    own_w[0:COLS, 0:COLS] = hi
    own_w[COLS:, 0:COLS] = hi
    own_w[0:COLS, COLS:] = lo
    own_w[COLS:, COLS:] = jnp.zeros_like(lo)
    edge_hi[...] = jnp.zeros_like(edge_hi)
    edge_lo[...] = jnp.zeros_like(edge_lo)
    for side in range(2):
        start = -REACH if side == 0 else COLS
        hi, lo = band(jnp.abs(iota((REACH, COLS), 0) + start - iota((REACH, COLS), 1)))
        for j in range(8):
            rows = slice(side * COLS + j * REACH, side * COLS + (j + 1) * REACH)
            edge_hi[rows, j * COLS : (j + 1) * COLS] = hi
            edge_lo[rows, j * COLS : (j + 1) * COLS] = lo


def kernel(
    members, grad, index, lat_taps, lon_taps, order, pack, spread, out,
    moved_m, tok, tile, sorted_t, moved_t, moved_i, lanes, grid, edge_m, edge_g, near_m, near_g,
    lat_hi, lat_lo, own_w, edge_hi, edge_lo, own_z, part,
    m_send, m_recv, t_send, t_recv, u_send, u_recv, i_send, i_recv, own_sem,
    g_send, g_recv, n_send, n_recv, r_send, r_recv,
):
    e, l, n = position()
    barrier = pltpu.get_barrier_semaphore()

    def greet(who):
        pl.semaphore_signal(barrier, inc=1, device_id=who, device_id_type=MESH)

    for de in (4, 3, 5, 2, 6, 1, 7, 0):
        for q in range(LAT):
            if de == 0:
                pl.when(l != q)(functools.partial(greet, (e, q, n)))
            else:
                greet((lax.rem(e + de, ENS), q, n))
    for dn in range(1, LON):
        greet((e, l, lax.rem(n + dn, LON)))

    lane = iota((16, COLS), 1) // PIECE
    row = iota((16, CHANNELS), 0)
    q, ch = row // 4, row % 4
    first = jnp.where(q == 0, 0, 3 * q + 1)
    ch = jnp.where(jnp.logical_and(q != 0, ch == 3), 2, ch)
    picks = (iota((16, CHANNELS), 1) == GROUP * e + first + ch).astype(F32).astype(BF16)
    mine = jnp.dot(picks, grad[...], preferred_element_type=F32)
    for g in range(4):
        tiles = [mine[:, (4 * q + g) * COLS : (4 * q + g + 1) * COLS] for q in range(LAT)]
        for j in range(4):
            total = jnp.zeros((16, COLS), F32)
            for q in range(LAT):
                turned = tiles[q] if q == j else pltpu.roll(tiles[q], (q - j) * PIECE % COLS, 1)
                total = jnp.where(lane == q, turned, total)
            tok[4 * g + j] = total.astype(BF16)
    wanted = index[...]
    moved_i[l] = (wanted >> 11) * PIECE + (wanted & 2047) - (l * LON + n) * PIECE
    tile[n] = tok[n]

    pl.semaphore_wait(barrier, ENS * LAT - 1 + LON - 1)

    def token_copy(dn):
        to = lax.rem(n + dn, LON)
        return remote(tok.at[to], tile.at[n], t_send.at[dn], t_recv.at[n], (e, l, to))

    def index_copy(q):
        return remote(moved_i.at[l], moved_i.at[l], i_send.at[q], i_recv.at[l], (e, q, n))

    def sorted_copy(q):
        return remote(sorted_t.at[q], moved_t.at[l], u_send.at[q], u_recv.at[l], (e, q, n))

    def member_refs(p, to, q):
        count = PART_COUNT[p][q]
        return (
            members.at[:, pl.ds(GROUP * to + FIRST[q] + PART_FIRST[p], count)],
            moved_m.at[pl.ds(2 * e, 2), pl.ds(PART_FIRST[p], count), l],
        )

    def member_copy(p, de, q):
        to = lax.rem(e + de, ENS)
        return remote(
            *member_refs(p, to, q), m_send.at[p, LAT * de + q], m_recv.at[p, LAT * e + l], (to, q, n)
        )

    def own_copy(p, q):
        return pltpu.make_async_copy(*member_refs(p, e, q), own_sem.at[p])

    def for_each(do, own=None):
        for de in (4, 3, 5, 2, 6, 1, 7, 0):
            for q in range(LAT):
                if de == 0:
                    pl.when(l != q)(functools.partial(do, de, q))
                    if own is not None:
                        pl.when(l == q)(functools.partial(own, q))
                else:
                    do(de, q)

    def others(do):
        for q in range(LAT):
            pl.when(l != q)(functools.partial(do, q))

    for dn in range(1, LON):
        token_copy(dn).start()
    others(lambda q: index_copy(q).start())
    for_each(lambda de, q: member_copy(0, de, q).start(), lambda q: own_copy(0, q).start())

    for dn in range(1, LON):
        frm = lax.rem(n + dn, LON)
        remote(tok.at[frm], tile.at[frm], t_send.at[dn], t_recv.at[frm], (e, l, frm)).wait_recv()
    flat = tile[...].reshape(LON * 16, COLS)
    sorted_t[...] = (
        jnp.dot(order[...], flat, preferred_element_type=F32).astype(BF16).reshape(LAT, 64, COLS)
    )
    moved_t[l] = sorted_t[l]
    others(lambda q: sorted_copy(q).start())

    matrices(lat_taps, lon_taps, lat_hi, lat_lo, own_w, edge_hi, edge_lo)

    def tokens_here(q):
        remote(sorted_t.at[q], moved_t.at[q], u_send.at[q], u_recv.at[q], (e, q, n)).wait_recv()
        remote(moved_i.at[q], moved_i.at[q], i_send.at[q], i_recv.at[q], (e, q, n)).wait_recv()
        sorted_copy(q).wait_send()
        index_copy(q).wait_send()

    others(tokens_here)
    for dn in range(1, LON):
        token_copy(dn).wait_send()

    parts = [moved_t[:, 16 * j : 16 * j + 16, :].astype(F32).reshape(64, COLS) for j in range(4)]
    lane = iota((64, COLS), 1) // PIECE
    for q in range(LAT):
        total = jnp.zeros((64, COLS), F32)
        for j in range(4):
            turned = parts[j] if j == q else pltpu.roll(parts[j], (j - q) * PIECE % COLS, 1)
            total = jnp.where(lane == j, turned, total)
        lanes[q] = total
    high = iota((8, COLS), 0) // 4

    @pl.loop(0, TALL)
    def _(i):
        q = i // ROWS
        offset = jnp.broadcast_to(moved_i[q, pl.ds(i % ROWS, 1), :], (8, COLS))
        which = (offset >> 7) - high
        at = offset & 127
        total = jnp.zeros((8, COLS), F32)
        for v in range(8):
            found = jnp.take_along_axis(lanes[q, 8 * v : 8 * v + 8, :], at, axis=1)
            total = jnp.where(which == 2 * v, found, total)
        total = total[0:4] + total[4:8]
        for c in range(SLOTS):
            grid[c, pl.ds(i, 1), :] = total[c : c + 1]

    for c in range(SLOTS):
        both = jnp.dot(grid[c].astype(BF16), spread[...], preferred_element_type=F32).astype(BF16)
        edge_g[0, c] = both[:, :COLS]
        edge_g[1, c] = both[:, COLS:]

    near = [(e, l, lax.rem(n + LON - 1, LON)), (e, l, lax.rem(n + 1, LON))]

    def grid_edge(side):
        return remote(edge_g.at[side], near_g.at[1 - side], g_send.at[side], g_recv.at[side], near[side])

    for side in range(2):
        grid_edge(side).start()

    def follow(de, q):
        member_copy(0, de, q).wait_send()
        member_copy(1, de, q).start()

    for_each(follow, lambda q: own_copy(1, q).start())

    def dot(a, b):
        return jnp.dot(a, b, preferred_element_type=F32)

    def member(c, m):
        return moved_m[m, c].reshape(TALL, COLS)

    def pack_edges(c, half):
        row = jnp.concatenate([member(c, 8 * half + j) for j in range(8)], axis=1)
        both = dot(row, pack[...]).astype(BF16)
        edge_m[0, 2 * c + half] = both[:, :COLS]
        edge_m[1, 2 * c + half] = both[:, COLS:]

    def own_columns(c, half):
        g = grid[c]
        his = []
        for j in range(8):
            hi, lo = split(member(c, 8 * half + j).astype(F32) * g)
            his.append(jnp.concatenate([hi, lo], axis=1))
        both = dot(jnp.concatenate(his, axis=0), own_w[...])
        own_z[c % 2, half] = both[:, :COLS] + both[:, COLS:]

    def finish(c, half):
        his, los = [], []
        for side in range(2):
            hi, lo = split(near_m[side, 2 * c + half].astype(F32) * near_g[side, c].astype(F32))
            his.append(hi)
            los.append(lo)
        hi, lo = jnp.concatenate(his, axis=1), jnp.concatenate(los, axis=1)
        outer = dot(hi, edge_hi[...]) + dot(lo, edge_hi[...]) + dot(hi, edge_lo[...])
        z_hi, z_lo = [], []
        for j in range(8):
            z = own_z[c % 2, half, j * TALL : (j + 1) * TALL] + outer[:, j * COLS : (j + 1) * COLS]
            hi, lo = split(z)
            z_hi.append(hi)
            z_lo.append(lo)

        def field_pairs(parts):
            return jnp.concatenate(
                [jnp.concatenate(parts[0:4], axis=0), jnp.concatenate(parts[4:8], axis=0)], axis=1
            )

        z_hi, z_lo = field_pairs(z_hi), field_pairs(z_lo)
        v = dot(lat_hi[...], z_hi) + dot(lat_lo[...], z_hi) + dot(lat_hi[...], z_lo)
        total = jnp.zeros((TALL, COLS), F32)
        for j in range(8):
            k = j % 4
            field = v[k * TALL : (k + 1) * TALL, (j // 4) * COLS : (j // 4 + 1) * COLS]
            total = total + member(c, 8 * half + j).astype(F32) * field
        return total

    def edge_copy(p, side, count):
        part_of = pl.ds(2 * PART_FIRST[p], 2 * count)
        return remote(
            edge_m.at[side, part_of], near_m.at[1 - side, part_of],
            n_send.at[p, side], n_recv.at[p, side], near[side],
        )

    def result_copy(p, q, count):
        return remote(
            part.at[q, pl.ds(PART_FIRST[p], count)],
            out.at[pl.ds(first_of(l) + PART_FIRST[p], count)],
            r_send.at[p, q], r_recv.at[p, l], (e, q, n),
        )

    def by_count(p, do):
        if PART_COUNT[p][0] == PART_COUNT[p][1]:
            do(PART_COUNT[p][0])
        else:
            pl.when(l == 0)(functools.partial(do, PART_COUNT[p][0]))
            pl.when(l != 0)(functools.partial(do, PART_COUNT[p][1]))

    def work(p, count):
        def arrived(de, q):
            frm = lax.rem(e + de, ENS)
            ref = moved_m.at[pl.ds(2 * frm, 2), pl.ds(PART_FIRST[p], count), q]
            remote(ref, ref, m_send.at[p, 0], m_recv.at[p, LAT * frm + q], (frm, q, n)).wait_recv()

        for_each(arrived, lambda q: own_copy(p, q).wait())
        slots = range(PART_FIRST[p], PART_FIRST[p] + count)
        for c in slots:
            for half in range(2):
                pack_edges(c, half)
        for side in range(2):
            edge_copy(p, side, count).start()
        for c in slots:
            for half in range(2):
                own_columns(c, half)
        for side in range(2):
            if p == 0:
                grid_edge(side).wait()
            edge_copy(p, side, count).wait()
        for c in slots:
            total = finish(c, 0) + finish(c, 1)
            for q in range(LAT):
                part[q, c] = total[q * ROWS : (q + 1) * ROWS]
        others(lambda q: result_copy(p, q, count).start())
        out[pl.ds(first_of(l) + PART_FIRST[p], count)] = part[l, pl.ds(PART_FIRST[p], count)]

    for p in range(2):
        by_count(p, functools.partial(work, p))

    for_each(lambda de, q: member_copy(1, de, q).wait_send())
    for p in range(2):

        def result_here(q, p=p):
            ref = out.at[pl.ds(FIRST[q] + PART_FIRST[p], PART_COUNT[p][q])]
            remote(ref, ref, r_send.at[p, q], r_recv.at[p, q], (e, q, n)).wait_recv()

        others(result_here)
        by_count(p, lambda count, p=p: others(lambda q: result_copy(p, q, count).wait_send()))


def increments(members, grad, index, lat_taps, lon_taps, order, pack, spread):
    dma = pltpu.SemaphoreType.DMA
    return pl.pallas_call(
        kernel,
        out_shape=jax.ShapeDtypeStruct((GROUP, ROWS, COLS), F32),
        in_specs=[ANY, VMEM, VMEM, SMEM, SMEM, VMEM, VMEM, VMEM],
        out_specs=VMEM,
        scratch_shapes=[
            pltpu.VMEM((2 * ENS, SLOTS, LAT, ROWS, COLS), BF16),
            pltpu.VMEM((LON, 16, COLS), BF16),
            pltpu.VMEM((LON, 16, COLS), BF16),
            pltpu.VMEM((LAT, 64, COLS), BF16),
            pltpu.VMEM((LAT, 64, COLS), BF16),
            pltpu.VMEM((LAT, ROWS, COLS), jnp.int32),
            pltpu.VMEM((LAT, 64, COLS), F32),
            pltpu.VMEM((SLOTS, TALL, COLS), F32),
            pltpu.VMEM((2, 2 * SLOTS, TALL, COLS), BF16),
            pltpu.VMEM((2, SLOTS, TALL, COLS), BF16),
            pltpu.VMEM((2, 2 * SLOTS, TALL, COLS), BF16),
            pltpu.VMEM((2, SLOTS, TALL, COLS), BF16),
            pltpu.VMEM((256, 256), BF16),
            pltpu.VMEM((256, 256), BF16),
            pltpu.VMEM((256, 256), BF16),
            pltpu.VMEM((256, 1024), BF16),
            pltpu.VMEM((256, 1024), BF16),
            pltpu.VMEM((2, 2, 8 * TALL, COLS), F32),
            pltpu.VMEM((LAT, SLOTS, ROWS, COLS), F32),
            dma((2, ENS * LAT)), dma((2, ENS * LAT)),
            dma((LON,)), dma((LON,)),
            dma((LAT,)), dma((LAT,)),
            dma((LAT,)), dma((LAT,)),
            dma((2,)),
            dma((2,)), dma((2,)),
            dma((2, 2)), dma((2, 2)),
            dma((2, LAT)), dma((2, LAT)),
        ],
        compiler_params=pltpu.CompilerParams(
            collective_id=0, has_side_effects=True, vmem_limit_bytes=48 * 2**20
        ),
    )(members, grad, index, lat_taps, lon_taps, order, pack, spread)


def selections():
    to, frm = jnp.arange(256)[:, None], jnp.arange(256)[None, :]
    q, j, g, ch = to // 64, to // 16 % 4, to // 4 % 4, to % 4
    order = (frm == (4 * g + j) * 16 + 4 * q + ch).astype(BF16)
    row, col = jnp.arange(1024)[:, None], jnp.arange(256)[None, :]
    side, j, cc = col // COLS, col % COLS // REACH, col % REACH
    edge = jnp.where(side == 0, cc, COLS - REACH + cc)
    pack = (row == j * COLS + edge).astype(BF16)
    spread = (jnp.arange(COLS)[:, None] == edge).astype(BF16)
    return order, pack, spread


def local(grad_tokens, token_index, members, lat_taps, lon_taps):
    order, pack, spread = selections()
    total = increments(members, grad_tokens, token_index, lat_taps, lon_taps, order, pack, spread)
    return total / (2 * ENS - 1)


def solution(mesh):
    in_specs = (P(None, ("lat", "lon")), P("lat", "lon"), P("ens", None, "lat", "lon"), P(), P())
    out_specs = P("ens", "lat", "lon")
    return jax.shard_map(local, mesh=mesh, in_specs=in_specs, out_specs=out_specs, check_vma=False)
```

```python
import functools

import jax
import jax.numpy as jnp
from jax import lax
from jax.experimental import pallas as pl
from jax.experimental.pallas import tpu as pltpu
from jax.sharding import PartitionSpec as P

MESH = pl.DeviceIdType.MESH
BF16, F32 = jnp.bfloat16, jnp.float32
CHANNELS = 104
GROUP = 13
SLOTS = 4
SPARE = 2
DEPTH = 16
OFFSETS = (8, 7, 9, 6, 10, 5, 11, 4, 12, 3, 13, 2, 14, 1, 15, 0)
ENS, LAT, LON = 8, 4, 16
ROWS, COLS = 16, 128
TALL = LAT * ROWS
HALO = 8
REACH = 2 * HALO
PIECE = 32
VMEM = pl.BlockSpec(memory_space=pltpu.VMEM)
ANY = pl.BlockSpec(memory_space=pl.ANY)
SMEM = pl.BlockSpec(memory_space=pltpu.SMEM)


def position():
    return lax.axis_index("ens"), lax.axis_index("lat"), lax.axis_index("lon")


def remote(src, dst, send, recv, device):
    return pltpu.make_async_remote_copy(
        src_ref=src, dst_ref=dst, send_sem=send, recv_sem=recv, device_id=device, device_id_type=MESH
    )


def first_of(lat):
    return jnp.where(lat == 0, 0, 3 * lat + 1)


def iota(shape, dim):
    return lax.broadcasted_iota(jnp.int32, shape, dim)


def split(x):
    hi = x.astype(BF16)
    return hi, (x - hi.astype(F32)).astype(BF16)


def matrices(lat_taps, lon_taps, lat_hi, lat_lo, own_w, edge_hi, edge_lo):
    taps = [lat_taps[p] for p in range(2 * HALO + 1)]
    shift = iota((TALL, TALL), 1) - iota((TALL, TALL), 0) + HALO
    once = jnp.zeros((TALL, TALL), F32)
    for p, tap in enumerate(taps):
        once = jnp.where(shift == p, tap, once)
    both = lax.dot_general(
        once, once, (((1,), (1,)), ((), ())), precision=lax.Precision.HIGHEST, preferred_element_type=F32
    )
    hi, lo = split(both)
    lat_hi[...] = jnp.zeros_like(lat_hi)
    lat_lo[...] = jnp.zeros_like(lat_lo)
    for j in range(4):
        lat_hi[j * TALL : (j + 1) * TALL, j * TALL : (j + 1) * TALL] = hi
        lat_lo[j * TALL : (j + 1) * TALL, j * TALL : (j + 1) * TALL] = lo
    taps = [lon_taps[p] for p in range(2 * HALO + 1)]
    twice = []
    for d in range(REACH + 1):
        total = taps[d] * taps[0]
        for a in range(d + 1, REACH + 1):
            total = total + taps[a] * taps[a - d]
        twice.append(total)

    def band(distance):
        out = jnp.zeros(distance.shape, F32)
        for d in range(REACH + 1):
            out = jnp.where(distance == d, twice[d], out)
        return split(out)

    hi, lo = band(jnp.abs(iota((COLS, COLS), 0) - iota((COLS, COLS), 1)))
    own_w[0:COLS, 0:COLS] = hi
    own_w[COLS:, 0:COLS] = hi
    own_w[0:COLS, COLS:] = lo
    own_w[COLS:, COLS:] = jnp.zeros_like(lo)
    edge_hi[...] = jnp.zeros_like(edge_hi)
    edge_lo[...] = jnp.zeros_like(edge_lo)
    for side in range(2):
        start = -REACH if side == 0 else COLS
        hi, lo = band(jnp.abs(iota((REACH, COLS), 0) + start - iota((REACH, COLS), 1)))
        for j in range(8):
            rows = slice(side * COLS + j * REACH, side * COLS + (j + 1) * REACH)
            edge_hi[rows, j * COLS : (j + 1) * COLS] = hi
            edge_lo[rows, j * COLS : (j + 1) * COLS] = lo


def token_order(order):
    to, frm = iota((256, 256), 0), iota((256, 256), 1)
    q, j, g, ch = to // 64, to // 16 % 4, to // 4 % 4, to % 4
    order[...] = (frm == (4 * g + j) * 16 + 4 * q + ch).astype(F32).astype(BF16)


def edge_selections(pack, spread):
    col = iota((COLS, 256), 1)
    side, j, cc = col // COLS, col % COLS // REACH, col % REACH
    edge = jnp.where(side == 0, cc, COLS - REACH + cc)
    hit = iota((COLS, 256), 0) == edge
    spread[...] = hit.astype(F32).astype(BF16)
    for k in range(8):
        here = jnp.logical_and(hit, j == k)
        pack[k * COLS : (k + 1) * COLS] = here.astype(F32).astype(BF16)


def kernel(
    members, grad, index, lat_taps, lon_taps, out,
    tokens_in, index_in, order, pack, spread, moved_m, tok, tile, sorted_t, moved_t, moved_i, lanes, grid, edge_m, edge_g, near_m, near_g,
    lat_hi, lat_lo, own_w, edge_hi, edge_lo, own_z, part,
    m_send, m_recv, s_send, s_recv, t_send, t_recv, u_send, u_recv, i_send, i_recv, own_sem,
    g_send, g_recv, n_send, n_recv, r_send, r_recv,
):
    e, l, n = position()
    core = lax.rem(l, 2)
    z = (l // 2) * ENS + e
    barrier = pltpu.get_barrier_semaphore()

    def along(d, kk):
        there = lax.rem(z + d, DEPTH)
        return lax.rem(there, ENS), 2 * (there // ENS) + lax.rem(core + kk, 2)

    def greet(who):
        pl.semaphore_signal(barrier, inc=1, device_id=who, device_id_type=MESH)

    pairs = [(d, kk) for d in OFFSETS for kk in range(2) if (d, kk) != (0, 0)]
    for d, kk in pairs:
        greet((*along(d, kk), n))
    for dn in range(1, LON):
        greet((e, l, lax.rem(n + dn, LON)))
    read_grad = pltpu.make_async_copy(grad, tokens_in, own_sem.at[3])
    read_index = pltpu.make_async_copy(index, index_in, own_sem.at[4])
    read_grad.start()
    read_index.start()

    pl.semaphore_wait(barrier, ENS * LAT - 1 + LON - 1)

    def token_copy(dn):
        to = lax.rem(n + dn, LON)
        return remote(tok.at[to], tile.at[n], t_send.at[dn], t_recv.at[n], (e, l, to))

    def index_copy(q):
        return remote(moved_i.at[l], moved_i.at[l], i_send.at[q], i_recv.at[l], (e, q, n))

    def sorted_copy(q):
        return remote(sorted_t.at[q], moved_t.at[l], u_send.at[q], u_recv.at[l], (e, q, n))

    def member_refs(p, to, q):
        slot, channel, count = ((0, 0, 2), (3, jnp.where(q == 0, 3, 2), 1), (SPARE, SPARE, 1))[p]
        return (
            members.at[:, pl.ds(GROUP * to + first_of(q) + channel, count)],
            moved_m.at[pl.ds(2 * e, 2), pl.ds(slot, count), l],
        )

    def member_copy(p, d, kk):
        to, q = along(d, kk)
        return remote(*member_refs(p, to, q), m_send.at[p, 2 * d + kk], m_recv.at[p, 2 * d + kk], (to, q, n))

    def member_here(p, d, kk):
        frm, q = along(DEPTH - d, kk)
        slot, count = ((0, 2), (3, 1))[p]
        ref = moved_m.at[pl.ds(2 * frm, 2), pl.ds(slot, count), q]
        return remote(ref, ref, m_send.at[p, 2 * d + kk], m_recv.at[p, 2 * d + kk], (frm, q, n))

    def own_copy(p):
        return pltpu.make_async_copy(*member_refs(p, e, l), own_sem.at[p])

    def send_part(p):
        for d, kk in pairs:
            member_copy(p, d, kk).start()
        own_copy(p).start()

    def spare_copy(de):
        to = lax.rem(e + de, ENS)
        return remote(*member_refs(2, to, 0), s_send.at[de], s_recv.at[de, l], (to, 0, n))

    def spare_here(de, q):
        frm = lax.rem(e + ENS - de, ENS)
        ref = moved_m.at[pl.ds(2 * frm, 2), pl.ds(SPARE, 1), q]
        return remote(ref, ref, s_send.at[de], s_recv.at[de, q], (frm, q, n))

    def own_spare():
        return pltpu.make_async_copy(*member_refs(2, e, 0), own_sem.at[2])

    def for_spares(do):
        for de in (4, 3, 5, 2, 6, 1, 7):
            do(de)
        pl.when(l != 0)(functools.partial(do, 0))

    def others(do):
        for q in range(LAT):
            pl.when(l != q)(functools.partial(do, q))

    send_part(0)
    lane = iota((16, COLS), 1) // PIECE
    row = iota((16, CHANNELS), 0)
    q, ch = row // 4, row % 4
    first = jnp.where(q == 0, 0, 3 * q + 1)
    ch = jnp.where(jnp.logical_and(q != 0, ch == 3), 2, ch)
    picks = (iota((16, CHANNELS), 1) == GROUP * e + first + ch).astype(F32).astype(BF16)
    read_grad.wait()
    read_index.wait()
    mine = jnp.dot(picks, tokens_in[...], preferred_element_type=F32)
    for g in range(4):
        tiles = [mine[:, (4 * q + g) * COLS : (4 * q + g + 1) * COLS] for q in range(LAT)]
        for j in range(4):
            total = jnp.zeros((16, COLS), F32)
            for q in range(LAT):
                turned = tiles[q] if q == j else pltpu.roll(tiles[q], (q - j) * PIECE % COLS, 1)
                total = jnp.where(lane == q, turned, total)
            tok[4 * g + j] = total.astype(BF16)
    wanted = index_in[...]
    moved_i[l] = (wanted >> 11) * PIECE + (wanted & 2047) - (l * LON + n) * PIECE
    tile[n] = tok[n]

    for dn in range(1, LON):
        token_copy(dn).start()
    others(lambda q: index_copy(q).start())

    token_order(order)
    for dn in range(1, LON):
        frm = lax.rem(n + dn, LON)
        remote(tok.at[frm], tile.at[frm], t_send.at[dn], t_recv.at[frm], (e, l, frm)).wait_recv()
    flat = tile[...].reshape(LON * 16, COLS)
    sorted_t[...] = (
        jnp.dot(order[...], flat, preferred_element_type=F32).astype(BF16).reshape(LAT, 64, COLS)
    )
    moved_t[l] = sorted_t[l]
    others(lambda q: sorted_copy(q).start())
    for_spares(lambda de: spare_copy(de).start())
    pl.when(l == 0)(lambda: own_spare().start())
    send_part(1)

    edge_selections(pack, spread)
    matrices(lat_taps, lon_taps, lat_hi, lat_lo, own_w, edge_hi, edge_lo)

    def tokens_here(q):
        remote(sorted_t.at[q], moved_t.at[q], u_send.at[q], u_recv.at[q], (e, q, n)).wait_recv()
        remote(moved_i.at[q], moved_i.at[q], i_send.at[q], i_recv.at[q], (e, q, n)).wait_recv()
        sorted_copy(q).wait_send()
        index_copy(q).wait_send()

    others(tokens_here)
    for dn in range(1, LON):
        token_copy(dn).wait_send()

    parts = [moved_t[:, 16 * j : 16 * j + 16, :].astype(F32).reshape(64, COLS) for j in range(4)]
    lane = iota((64, COLS), 1) // PIECE
    for q in range(LAT):
        total = jnp.zeros((64, COLS), F32)
        for j in range(4):
            turned = parts[j] if j == q else pltpu.roll(parts[j], (j - q) * PIECE % COLS, 1)
            total = jnp.where(lane == j, turned, total)
        lanes[q] = total
    high = iota((8, COLS), 0) // 4

    @pl.loop(0, TALL, unroll=8)
    def _(i):
        q = i // ROWS
        offset = jnp.broadcast_to(moved_i[q, pl.ds(i % ROWS, 1), :], (8, COLS))
        which = (offset >> 7) - high
        at = offset & 127
        total = jnp.zeros((8, COLS), F32)
        for v in range(8):
            found = jnp.take_along_axis(lanes[q, 8 * v : 8 * v + 8, :], at, axis=1)
            total = jnp.where(which == 2 * v, found, total)
        total = total[0:4] + total[4:8]
        for c in range(SLOTS):
            grid[c, pl.ds(i, 1), :] = total[c : c + 1]

    for c in range(SLOTS):
        both = jnp.dot(grid[c].astype(BF16), spread[...], preferred_element_type=F32).astype(BF16)
        edge_g[0, c] = both[:, :COLS]
        edge_g[1, c] = both[:, COLS:]

    near = [(e, l, lax.rem(n + LON - 1, LON)), (e, l, lax.rem(n + 1, LON))]

    def grid_edge(side):
        return remote(edge_g.at[side], near_g.at[1 - side], g_send.at[side], g_recv.at[side], near[side])

    for side in range(2):
        grid_edge(side).start()

    def dot(a, b):
        return jnp.dot(a, b, preferred_element_type=F32)

    def member(c, m):
        return moved_m[m, c].reshape(TALL, COLS)

    def pack_edges(c, half):
        row = jnp.concatenate([member(c, 8 * half + j) for j in range(8)], axis=1)
        both = dot(row, pack[...]).astype(BF16)
        edge_m[0, 2 * c + half] = both[:, :COLS]
        edge_m[1, 2 * c + half] = both[:, COLS:]

    def own_columns(c, half):
        g = grid[c]
        his = []
        for j in range(8):
            hi, lo = split(member(c, 8 * half + j).astype(F32) * g)
            his.append(jnp.concatenate([hi, lo], axis=1))
        both = dot(jnp.concatenate(his, axis=0), own_w[...])
        own_z[c, half] = both[:, :COLS] + both[:, COLS:]

    def finish(c, half):
        his, los = [], []
        for side in range(2):
            hi, lo = split(near_m[side, 2 * c + half].astype(F32) * near_g[side, c].astype(F32))
            his.append(hi)
            los.append(lo)
        hi, lo = jnp.concatenate(his, axis=1), jnp.concatenate(los, axis=1)
        outer = dot(hi, edge_hi[...]) + dot(lo, edge_hi[...]) + dot(hi, edge_lo[...])
        z_hi, z_lo = [], []
        for j in range(8):
            z = own_z[c, half, j * TALL : (j + 1) * TALL] + outer[:, j * COLS : (j + 1) * COLS]
            hi, lo = split(z)
            z_hi.append(hi)
            z_lo.append(lo)

        def field_pairs(parts):
            return jnp.concatenate(
                [jnp.concatenate(parts[0:4], axis=0), jnp.concatenate(parts[4:8], axis=0)], axis=1
            )

        z_hi, z_lo = field_pairs(z_hi), field_pairs(z_lo)
        v = dot(lat_hi[...], z_hi) + dot(lat_lo[...], z_hi) + dot(lat_hi[...], z_lo)
        total = jnp.zeros((TALL, COLS), F32)
        for j in range(8):
            k = j % 4
            field = v[k * TALL : (k + 1) * TALL, (j // 4) * COLS : (j // 4 + 1) * COLS]
            total = total + member(c, 8 * half + j).astype(F32) * field
        return total

    def edge_copy(p, side):
        part_of = (pl.ds(0, 4), pl.ds(6, 2), pl.ds(4, 2))[p]
        return remote(
            edge_m.at[side, part_of], near_m.at[1 - side, part_of],
            n_send.at[p, side], n_recv.at[p, side], near[side],
        )

    def result_refs(p, frm, to):
        slot, channel, count = ((0, 0, 2), (3, jnp.where(frm == 0, 3, 2), 1), (SPARE, SPARE, 1))[p]
        return part.at[to, pl.ds(slot, count)], out.at[pl.ds(first_of(frm) + channel, count)]

    def result_copy(p, q):
        return remote(*result_refs(p, l, q), r_send.at[p, q], r_recv.at[p, l], (e, q, n))

    def result_here(p, q):
        ref = result_refs(p, jnp.int32(q), l)[1]
        return remote(ref, ref, r_send.at[p, q], r_recv.at[p, q], (e, q, n))

    def begin(p, slots):
        for c in slots:
            for half in range(2):
                pack_edges(c, half)
        for side in range(2):
            edge_copy(p, side).start()

    def middle(slots):
        for c in slots:
            for half in range(2):
                own_columns(c, half)

    def complete(p, slots):
        for side in range(2):
            edge_copy(p, side).wait()
        for c in slots:
            total = finish(c, 0) + finish(c, 1)
            for q in range(LAT):
                part[q, c] = total[q * ROWS : (q + 1) * ROWS]
        others(lambda q: result_copy(p, q).start())
        to = result_refs(p, l, l)[1]
        to[...] = part[l, slots[0] : slots[-1] + 1]

    for d, kk in pairs:
        member_here(0, d, kk).wait_recv()
    own_copy(0).wait()
    begin(0, (0, 1))

    @pl.when(l == 0)
    def _():
        for de in range(ENS):
            for q in range(LAT):
                if (de, q) != (0, 0):
                    spare_here(de, q).wait_recv()
        own_spare().wait()
        begin(2, (SPARE,))

    middle((0, 1))
    for side in range(2):
        grid_edge(side).wait()
    for d, kk in pairs:
        member_here(1, d, kk).wait_recv()
    own_copy(1).wait()
    begin(1, (3,))
    complete(0, (0, 1))

    @pl.when(l == 0)
    def _():
        middle((SPARE,))
        complete(2, (SPARE,))

    middle((3,))
    for p in range(2):
        for d, kk in pairs:
            member_copy(p, d, kk).wait_send()
    for_spares(lambda de: spare_copy(de).wait_send())
    complete(1, (3,))
    for p in range(2):
        others(lambda q, p=p: result_here(p, q).wait_recv())
        others(lambda q, p=p: result_copy(p, q).wait_send())
    pl.when(l != 0)(lambda: result_here(2, 0).wait_recv())

    @pl.when(l == 0)
    def _():
        others(lambda q: result_copy(2, q).wait_send())


def increments(members, grad, index, lat_taps, lon_taps):
    dma = pltpu.SemaphoreType.DMA
    return pl.pallas_call(
        kernel,
        out_shape=jax.ShapeDtypeStruct((GROUP, ROWS, COLS), F32),
        in_specs=[ANY, ANY, ANY, SMEM, SMEM],
        out_specs=VMEM,
        scratch_shapes=[
            pltpu.VMEM((CHANNELS, ROWS * COLS), BF16),
            pltpu.VMEM((ROWS, COLS), jnp.int32),
            pltpu.VMEM((256, 256), BF16),
            pltpu.VMEM((1024, 256), BF16),
            pltpu.VMEM((COLS, 256), BF16),
            pltpu.VMEM((2 * ENS, SLOTS, LAT, ROWS, COLS), BF16),
            pltpu.VMEM((LON, 16, COLS), BF16),
            pltpu.VMEM((LON, 16, COLS), BF16),
            pltpu.VMEM((LAT, 64, COLS), BF16),
            pltpu.VMEM((LAT, 64, COLS), BF16),
            pltpu.VMEM((LAT, ROWS, COLS), jnp.int32),
            pltpu.VMEM((LAT, 64, COLS), F32),
            pltpu.VMEM((SLOTS, TALL, COLS), F32),
            pltpu.VMEM((2, 2 * SLOTS, TALL, COLS), BF16),
            pltpu.VMEM((2, SLOTS, TALL, COLS), BF16),
            pltpu.VMEM((2, 2 * SLOTS, TALL, COLS), BF16),
            pltpu.VMEM((2, SLOTS, TALL, COLS), BF16),
            pltpu.VMEM((256, 256), BF16),
            pltpu.VMEM((256, 256), BF16),
            pltpu.VMEM((256, 256), BF16),
            pltpu.VMEM((256, 1024), BF16),
            pltpu.VMEM((256, 1024), BF16),
            pltpu.VMEM((SLOTS, 2, 8 * TALL, COLS), F32),
            pltpu.VMEM((LAT, SLOTS, ROWS, COLS), F32),
            dma((2, 2 * DEPTH)), dma((2, 2 * DEPTH)),
            dma((ENS,)), dma((ENS, LAT)),
            dma((LON,)), dma((LON,)),
            dma((LAT,)), dma((LAT,)),
            dma((LAT,)), dma((LAT,)),
            dma((5,)),
            dma((2,)), dma((2,)),
            dma((3, 2)), dma((3, 2)),
            dma((3, LAT)), dma((3, LAT)),
        ],
        compiler_params=pltpu.CompilerParams(
            collective_id=0, has_side_effects=True, vmem_limit_bytes=60 * 2**20
        ),
    )(members, grad, index, lat_taps, lon_taps)


def local(grad_tokens, token_index, members, lat_taps, lon_taps):
    total = increments(members, grad_tokens, token_index, lat_taps, lon_taps)
    return total / (2 * ENS - 1)


def solution(mesh):
    in_specs = (P(None, ("lat", "lon")), P("lat", "lon"), P("ens", None, "lat", "lon"), P(), P())
    out_specs = P("ens", "lat", "lon")
    return jax.shard_map(local, mesh=mesh, in_specs=in_specs, out_specs=out_specs, check_vma=False)
```

```python
import functools

import jax
import jax.numpy as jnp
from jax import lax
from jax.experimental import pallas as pl
from jax.experimental.pallas import tpu as pltpu
from jax.sharding import PartitionSpec as P

MESH = pl.DeviceIdType.MESH
BF16, F32 = jnp.bfloat16, jnp.float32
CHANNELS = 104
GROUP = 13
SLOTS = 4
SPARE = 2
DEPTH = 16
OFFSETS = (8, 7, 9, 6, 10, 5, 11, 4, 12, 3, 13, 2, 14, 1, 15, 0)
ENS, LAT, LON = 8, 4, 16
ROWS, COLS = 16, 128
TALL = LAT * ROWS
HALO = 8
REACH = 2 * HALO
PIECE = 32
VMEM = pl.BlockSpec(memory_space=pltpu.VMEM)
ANY = pl.BlockSpec(memory_space=pl.ANY)
SMEM = pl.BlockSpec(memory_space=pltpu.SMEM)


def position():
    return lax.axis_index("ens"), lax.axis_index("lat"), lax.axis_index("lon")


def remote(src, dst, send, recv, device):
    return pltpu.make_async_remote_copy(
        src_ref=src, dst_ref=dst, send_sem=send, recv_sem=recv, device_id=device, device_id_type=MESH
    )


def first_of(lat):
    return jnp.where(lat == 0, 0, 3 * lat + 1)


def iota(shape, dim):
    return lax.broadcasted_iota(jnp.int32, shape, dim)


def split(x):
    hi = x.astype(BF16)
    return hi, (x - hi.astype(F32)).astype(BF16)


def matrices(lat_taps, lon_taps, lat_hi, lat_lo, own_w, edge_hi, edge_lo):
    taps = [lat_taps[p] for p in range(2 * HALO + 1)]
    shift = iota((TALL, TALL), 1) - iota((TALL, TALL), 0) + HALO
    once = jnp.zeros((TALL, TALL), F32)
    for p, tap in enumerate(taps):
        once = jnp.where(shift == p, tap, once)
    both = lax.dot_general(
        once, once, (((1,), (1,)), ((), ())), precision=lax.Precision.HIGHEST, preferred_element_type=F32
    )
    hi, lo = split(both)
    lat_hi[...] = jnp.zeros_like(lat_hi)
    lat_lo[...] = jnp.zeros_like(lat_lo)
    for j in range(4):
        lat_hi[j * TALL : (j + 1) * TALL, j * TALL : (j + 1) * TALL] = hi
        lat_lo[j * TALL : (j + 1) * TALL, j * TALL : (j + 1) * TALL] = lo
    taps = [lon_taps[p] for p in range(2 * HALO + 1)]
    twice = []
    for d in range(REACH + 1):
        total = taps[d] * taps[0]
        for a in range(d + 1, REACH + 1):
            total = total + taps[a] * taps[a - d]
        twice.append(total)

    def band(distance):
        out = jnp.zeros(distance.shape, F32)
        for d in range(REACH + 1):
            out = jnp.where(distance == d, twice[d], out)
        return split(out)

    hi, lo = band(jnp.abs(iota((COLS, COLS), 0) - iota((COLS, COLS), 1)))
    own_w[0:COLS, 0:COLS] = hi
    own_w[COLS:, 0:COLS] = hi
    own_w[0:COLS, COLS:] = lo
    own_w[COLS:, COLS:] = jnp.zeros_like(lo)
    edge_hi[...] = jnp.zeros_like(edge_hi)
    edge_lo[...] = jnp.zeros_like(edge_lo)
    for side in range(2):
        start = -REACH if side == 0 else COLS
        hi, lo = band(jnp.abs(iota((REACH, COLS), 0) + start - iota((REACH, COLS), 1)))
        for j in range(8):
            rows = slice(side * COLS + j * REACH, side * COLS + (j + 1) * REACH)
            edge_hi[rows, j * COLS : (j + 1) * COLS] = hi
            edge_lo[rows, j * COLS : (j + 1) * COLS] = lo


def token_order(order):
    to, frm = iota((256, 256), 0), iota((256, 256), 1)
    q, j, g, ch = to // 64, to // 16 % 4, to // 4 % 4, to % 4
    order[...] = (frm == (4 * g + j) * 16 + 4 * q + ch).astype(F32).astype(BF16)


def edge_selections(pack, spread):
    col = iota((COLS, 256), 1)
    side, j, cc = col // COLS, col % COLS // REACH, col % REACH
    edge = jnp.where(side == 0, cc, COLS - REACH + cc)
    hit = iota((COLS, 256), 0) == edge
    spread[...] = hit.astype(F32).astype(BF16)
    for k in range(8):
        here = jnp.logical_and(hit, j == k)
        pack[k * COLS : (k + 1) * COLS] = here.astype(F32).astype(BF16)


def kernel(
    members, grad, index, lat_taps, lon_taps, out,
    tokens_in, index_in, order, pack, spread, moved_m, tok, tile, sorted_t, moved_t, moved_i, lanes, grid, edge_m, edge_g, near_m, near_g,
    lat_hi, lat_lo, own_w, edge_hi, edge_lo, own_z, part,
    m_send, m_recv, s_send, s_recv, t_send, t_recv, u_send, u_recv, i_send, i_recv, own_sem,
    g_send, g_recv, n_send, n_recv, r_send, r_recv,
):
    e, l, n = position()
    core = lax.rem(l, 2)
    z = (l // 2) * ENS + e
    barrier = pltpu.get_barrier_semaphore()

    def along(d, kk):
        there = lax.rem(z + d, DEPTH)
        return lax.rem(there, ENS), 2 * (there // ENS) + lax.rem(core + kk, 2)

    def greet(who):
        pl.semaphore_signal(barrier, inc=1, device_id=who, device_id_type=MESH)

    pairs = [(d, kk) for d in OFFSETS for kk in range(2) if (d, kk) != (0, 0)]
    for d, kk in pairs:
        greet((*along(d, kk), n))
    for dn in range(1, LON):
        greet((e, l, lax.rem(n + dn, LON)))
    read_grad = pltpu.make_async_copy(grad, tokens_in, own_sem.at[3])
    read_index = pltpu.make_async_copy(index, index_in, own_sem.at[4])
    read_grad.start()
    read_index.start()

    pl.semaphore_wait(barrier, ENS * LAT - 1 + LON - 1)

    def token_copy(dn):
        to = lax.rem(n + dn, LON)
        return remote(tok.at[to], tile.at[n], t_send.at[dn], t_recv.at[n], (e, l, to))

    def index_copy(q):
        return remote(moved_i.at[l], moved_i.at[l], i_send.at[q], i_recv.at[l], (e, q, n))

    def sorted_copy(q):
        return remote(sorted_t.at[q], moved_t.at[l], u_send.at[q], u_recv.at[l], (e, q, n))

    def member_refs(p, to, q):
        slot, channel, count = ((0, 0, 2), (3, jnp.where(q == 0, 3, 2), 1), (SPARE, SPARE, 1))[p]
        return (
            members.at[:, pl.ds(GROUP * to + first_of(q) + channel, count)],
            moved_m.at[pl.ds(2 * e, 2), pl.ds(slot, count), l],
        )

    def member_copy(p, d, kk):
        to, q = along(d, kk)
        return remote(*member_refs(p, to, q), m_send.at[p, 2 * d + kk], m_recv.at[p, 2 * d + kk], (to, q, n))

    def member_here(p, d, kk):
        frm, q = along(DEPTH - d, kk)
        slot, count = ((0, 2), (3, 1))[p]
        ref = moved_m.at[pl.ds(2 * frm, 2), pl.ds(slot, count), q]
        return remote(ref, ref, m_send.at[p, 2 * d + kk], m_recv.at[p, 2 * d + kk], (frm, q, n))

    def own_copy(p):
        return pltpu.make_async_copy(*member_refs(p, e, l), own_sem.at[p])

    def send_part(p):
        for d, kk in pairs:
            member_copy(p, d, kk).start()
        own_copy(p).start()

    def spare_copy(de):
        to = lax.rem(e + de, ENS)
        return remote(*member_refs(2, to, 0), s_send.at[de], s_recv.at[de, l], (to, 0, n))

    def spare_here(de, q):
        frm = lax.rem(e + ENS - de, ENS)
        ref = moved_m.at[pl.ds(2 * frm, 2), pl.ds(SPARE, 1), q]
        return remote(ref, ref, s_send.at[de], s_recv.at[de, q], (frm, q, n))

    def own_spare():
        return pltpu.make_async_copy(*member_refs(2, e, 0), own_sem.at[2])

    def for_spares(do):
        for de in (4, 3, 5, 2, 6, 1, 7):
            do(de)
        pl.when(l != 0)(functools.partial(do, 0))

    def others(do):
        for q in range(LAT):
            pl.when(l != q)(functools.partial(do, q))

    send_part(0)
    lane = iota((16, COLS), 1) // PIECE
    row = iota((16, CHANNELS), 0)
    q, ch = row // 4, row % 4
    first = jnp.where(q == 0, 0, 3 * q + 1)
    ch = jnp.where(jnp.logical_and(q != 0, ch == 3), 2, ch)
    picks = (iota((16, CHANNELS), 1) == GROUP * e + first + ch).astype(F32).astype(BF16)
    read_grad.wait()
    read_index.wait()
    mine = jnp.dot(picks, tokens_in[...], preferred_element_type=F32)
    for g in range(4):
        tiles = [mine[:, (4 * q + g) * COLS : (4 * q + g + 1) * COLS] for q in range(LAT)]
        for j in range(4):
            total = jnp.zeros((16, COLS), F32)
            for q in range(LAT):
                turned = tiles[q] if q == j else pltpu.roll(tiles[q], (q - j) * PIECE % COLS, 1)
                total = jnp.where(lane == q, turned, total)
            tok[4 * g + j] = total.astype(BF16)
    wanted = index_in[...]
    moved_i[l] = (wanted >> 11) * PIECE + (wanted & 2047) - (l * LON + n) * PIECE
    tile[n] = tok[n]

    for dn in range(1, LON):
        token_copy(dn).start()
    others(lambda q: index_copy(q).start())

    token_order(order)
    for dn in range(1, LON):
        frm = lax.rem(n + dn, LON)
        remote(tok.at[frm], tile.at[frm], t_send.at[dn], t_recv.at[frm], (e, l, frm)).wait_recv()
    flat = tile[...].reshape(LON * 16, COLS)
    sorted_t[...] = (
        jnp.dot(order[...], flat, preferred_element_type=F32).astype(BF16).reshape(LAT, 64, COLS)
    )
    moved_t[l] = sorted_t[l]
    others(lambda q: sorted_copy(q).start())
    for_spares(lambda de: spare_copy(de).start())
    pl.when(l == 0)(lambda: own_spare().start())
    send_part(1)

    edge_selections(pack, spread)
    matrices(lat_taps, lon_taps, lat_hi, lat_lo, own_w, edge_hi, edge_lo)

    def tokens_here(q):
        remote(sorted_t.at[q], moved_t.at[q], u_send.at[q], u_recv.at[q], (e, q, n)).wait_recv()
        remote(moved_i.at[q], moved_i.at[q], i_send.at[q], i_recv.at[q], (e, q, n)).wait_recv()

    others(tokens_here)

    parts = [moved_t[:, 16 * j : 16 * j + 16, :].astype(F32).reshape(64, COLS) for j in range(4)]
    lane = iota((64, COLS), 1) // PIECE
    for q in range(LAT):
        total = jnp.zeros((64, COLS), F32)
        for j in range(4):
            turned = parts[j] if j == q else pltpu.roll(parts[j], (j - q) * PIECE % COLS, 1)
            total = jnp.where(lane == j, turned, total)
        lanes[q] = total
    high = iota((8, COLS), 0) // 4

    @pl.loop(0, TALL, unroll=8)
    def _(i):
        q = i // ROWS
        offset = jnp.broadcast_to(moved_i[q, pl.ds(i % ROWS, 1), :], (8, COLS))
        which = (offset >> 7) - high
        at = offset & 127
        total = jnp.zeros((8, COLS), F32)
        for v in range(8):
            found = jnp.take_along_axis(lanes[q, 8 * v : 8 * v + 8, :], at, axis=1)
            total = jnp.where(which == 2 * v, found, total)
        total = total[0:4] + total[4:8]
        for c in range(SLOTS):
            grid[c, pl.ds(i, 1), :] = total[c : c + 1]

    for c in range(SLOTS):
        both = jnp.dot(grid[c].astype(BF16), spread[...], preferred_element_type=F32).astype(BF16)
        edge_g[0, c] = both[:, :COLS]
        edge_g[1, c] = both[:, COLS:]

    near = [(e, l, lax.rem(n + LON - 1, LON)), (e, l, lax.rem(n + 1, LON))]

    def grid_edge(side):
        return remote(edge_g.at[side], near_g.at[1 - side], g_send.at[side], g_recv.at[side], near[side])

    for side in range(2):
        grid_edge(side).start()

    def dot(a, b):
        return jnp.dot(a, b, preferred_element_type=F32)

    def member(c, m):
        return moved_m[m, c].reshape(TALL, COLS)

    def pack_edges(c, half):
        row = jnp.concatenate([member(c, 8 * half + j) for j in range(8)], axis=1)
        both = dot(row, pack[...]).astype(BF16)
        edge_m[0, 2 * c + half] = both[:, :COLS]
        edge_m[1, 2 * c + half] = both[:, COLS:]

    def own_columns(c, half):
        g = grid[c]
        his = []
        for j in range(8):
            hi, lo = split(member(c, 8 * half + j).astype(F32) * g)
            his.append(jnp.concatenate([hi, lo], axis=1))
        both = dot(jnp.concatenate(his, axis=0), own_w[...])
        own_z[c, half] = both[:, :COLS] + both[:, COLS:]

    def finish(c, half):
        his, los = [], []
        for side in range(2):
            hi, lo = split(near_m[side, 2 * c + half].astype(F32) * near_g[side, c].astype(F32))
            his.append(hi)
            los.append(lo)
        hi, lo = jnp.concatenate(his, axis=1), jnp.concatenate(los, axis=1)
        outer = dot(hi, edge_hi[...]) + dot(lo, edge_hi[...]) + dot(hi, edge_lo[...])
        z_hi, z_lo = [], []
        for j in range(8):
            z = own_z[c, half, j * TALL : (j + 1) * TALL] + outer[:, j * COLS : (j + 1) * COLS]
            hi, lo = split(z)
            z_hi.append(hi)
            z_lo.append(lo)

        def field_pairs(parts):
            return jnp.concatenate(
                [jnp.concatenate(parts[0:4], axis=0), jnp.concatenate(parts[4:8], axis=0)], axis=1
            )

        z_hi, z_lo = field_pairs(z_hi), field_pairs(z_lo)
        v = dot(lat_hi[...], z_hi) + dot(lat_lo[...], z_hi) + dot(lat_hi[...], z_lo)
        total = jnp.zeros((TALL, COLS), F32)
        for j in range(8):
            k = j % 4
            field = v[k * TALL : (k + 1) * TALL, (j // 4) * COLS : (j // 4 + 1) * COLS]
            total = total + member(c, 8 * half + j).astype(F32) * field
        return total

    def edge_copy(p, side):
        part_of = (pl.ds(0, 4), pl.ds(6, 2), pl.ds(4, 2))[p]
        return remote(
            edge_m.at[side, part_of], near_m.at[1 - side, part_of],
            n_send.at[p, side], n_recv.at[p, side], near[side],
        )

    def result_refs(p, frm, to):
        slot, channel, count = ((0, 0, 2), (3, jnp.where(frm == 0, 3, 2), 1), (SPARE, SPARE, 1))[p]
        return part.at[to, pl.ds(slot, count)], out.at[pl.ds(first_of(frm) + channel, count)]

    def result_copy(p, q):
        return remote(*result_refs(p, l, q), r_send.at[p, q], r_recv.at[p, l], (e, q, n))

    def result_here(p, q):
        ref = result_refs(p, jnp.int32(q), l)[1]
        return remote(ref, ref, r_send.at[p, q], r_recv.at[p, q], (e, q, n))

    def begin(p, slots):
        for c in slots:
            for half in range(2):
                pack_edges(c, half)
        for side in range(2):
            edge_copy(p, side).start()

    def middle(slots):
        for c in slots:
            for half in range(2):
                own_columns(c, half)

    def complete(p, slots):
        for side in range(2):
            edge_copy(p, side).wait()
        for c in slots:
            total = finish(c, 0) + finish(c, 1)
            for q in range(LAT):
                part[q, c] = total[q * ROWS : (q + 1) * ROWS]
        others(lambda q: result_copy(p, q).start())
        to = result_refs(p, l, l)[1]
        to[...] = part[l, slots[0] : slots[-1] + 1]

    for d, kk in pairs:
        member_here(0, d, kk).wait_recv()
    own_copy(0).wait()
    begin(0, (0, 1))

    @pl.when(l == 0)
    def _():
        for de in range(ENS):
            for q in range(LAT):
                if (de, q) != (0, 0):
                    spare_here(de, q).wait_recv()
        own_spare().wait()
        begin(2, (SPARE,))

    middle((0, 1))
    for side in range(2):
        grid_edge(side).wait()
    for d, kk in pairs:
        member_here(1, d, kk).wait_recv()
    own_copy(1).wait()
    begin(1, (3,))
    complete(0, (0, 1))

    @pl.when(l == 0)
    def _():
        middle((SPARE,))
        complete(2, (SPARE,))

    middle((3,))
    complete(1, (3,))
    for p in range(2):
        for d, kk in pairs:
            member_copy(p, d, kk).wait_send()
    for_spares(lambda de: spare_copy(de).wait_send())
    for dn in range(1, LON):
        token_copy(dn).wait_send()
    others(lambda q: sorted_copy(q).wait_send())
    others(lambda q: index_copy(q).wait_send())
    for p in range(2):
        others(lambda q, p=p: result_here(p, q).wait_recv())
        others(lambda q, p=p: result_copy(p, q).wait_send())
    pl.when(l != 0)(lambda: result_here(2, 0).wait_recv())

    @pl.when(l == 0)
    def _():
        others(lambda q: result_copy(2, q).wait_send())


def increments(members, grad, index, lat_taps, lon_taps):
    dma = pltpu.SemaphoreType.DMA
    return pl.pallas_call(
        kernel,
        out_shape=jax.ShapeDtypeStruct((GROUP, ROWS, COLS), F32),
        in_specs=[ANY, ANY, ANY, SMEM, SMEM],
        out_specs=VMEM,
        scratch_shapes=[
            pltpu.VMEM((CHANNELS, ROWS * COLS), BF16),
            pltpu.VMEM((ROWS, COLS), jnp.int32),
            pltpu.VMEM((256, 256), BF16),
            pltpu.VMEM((1024, 256), BF16),
            pltpu.VMEM((COLS, 256), BF16),
            pltpu.VMEM((2 * ENS, SLOTS, LAT, ROWS, COLS), BF16),
            pltpu.VMEM((LON, 16, COLS), BF16),
            pltpu.VMEM((LON, 16, COLS), BF16),
            pltpu.VMEM((LAT, 64, COLS), BF16),
            pltpu.VMEM((LAT, 64, COLS), BF16),
            pltpu.VMEM((LAT, ROWS, COLS), jnp.int32),
            pltpu.VMEM((LAT, 64, COLS), F32),
            pltpu.VMEM((SLOTS, TALL, COLS), F32),
            pltpu.VMEM((2, 2 * SLOTS, TALL, COLS), BF16),
            pltpu.VMEM((2, SLOTS, TALL, COLS), BF16),
            pltpu.VMEM((2, 2 * SLOTS, TALL, COLS), BF16),
            pltpu.VMEM((2, SLOTS, TALL, COLS), BF16),
            pltpu.VMEM((256, 256), BF16),
            pltpu.VMEM((256, 256), BF16),
            pltpu.VMEM((256, 256), BF16),
            pltpu.VMEM((256, 1024), BF16),
            pltpu.VMEM((256, 1024), BF16),
            pltpu.VMEM((SLOTS, 2, 8 * TALL, COLS), F32),
            pltpu.VMEM((LAT, SLOTS, ROWS, COLS), F32),
            dma((2, 2 * DEPTH)), dma((2, 2 * DEPTH)),
            dma((ENS,)), dma((ENS, LAT)),
            dma((LON,)), dma((LON,)),
            dma((LAT,)), dma((LAT,)),
            dma((LAT,)), dma((LAT,)),
            dma((5,)),
            dma((2,)), dma((2,)),
            dma((3, 2)), dma((3, 2)),
            dma((3, LAT)), dma((3, LAT)),
        ],
        compiler_params=pltpu.CompilerParams(
            collective_id=0, has_side_effects=True, vmem_limit_bytes=60 * 2**20
        ),
    )(members, grad, index, lat_taps, lon_taps)


def local(grad_tokens, token_index, members, lat_taps, lon_taps):
    total = increments(members, grad_tokens, token_index, lat_taps, lon_taps)
    return total / (2 * ENS - 1)


def solution(mesh):
    in_specs = (P(None, ("lat", "lon")), P("lat", "lon"), P("ens", None, "lat", "lon"), P(), P())
    out_specs = P("ens", "lat", "lon")
    return jax.shard_map(local, mesh=mesh, in_specs=in_specs, out_specs=out_specs, check_vma=False)
```
